32 devices in a mesh: pole: 2 (over x), row: 8 (over z, y), leaf: 2 (over core).
Axes of the slice: x: 2, y: 2, z: 4, core: 2. Of those that a mesh axis runs over, the one named last changes fastest.
Arguments:
- ancestor_inverse: float32 [4, 2, 8192, 4096], P('pole', 'leaf', 'row'), parts along dimension 0, may hold values from -6 to 6
- panel: float32 [4, 2, 4096, 512], P('pole', 'leaf', 'row'), parts along dimension 0, may hold values from -0.0625 to 0.0625
- diagonal_inverse: float32 [4, 2, 256, 256], P('pole', 'leaf'), parts along dimension 0, may hold values from -6 to 6
- pattern: int32 [64, 2], replicated, may hold values 0 or 1
Outputs:
- offdiag_inverse: float32 [4, 8192, 512], P('pole', 'row', 'leaf'), parts along dimension 0
- diag_inverse: float32 [4, 2, 256, 256], P('pole', 'leaf'), parts along dimension 0
The draws below stay inside these ranges and needn't reach their ends.
There are 2 independent parts, one for each index of `pole`. The reference program is written for one: setup_inputs(seed, part) draws one part's arguments, and reference() takes and returns one part's arrays. A program takes and returns all parts, laid end to end along the dimension named above; an argument that names none is the same for every part. Nothing has to cross between parts.
All inputs are finite; a program needn't handle non-finite values.
Results may differ from the reference program's by a relative error of at most 0.0001.
Values sent between devices are 32-bit elements; how exact they have to be, the bound alone decides.
No kernel may reach another device: no remote copies, remote signals or barrier semaphores. Data moves between devices by JAX's collectives and lax.ppermute only.
A program may use at most 128 MiB of HBM per device.

```python
import jax
import jax.numpy as jnp
from jax import lax

ANC = 8192
WIDTH = 256
BLOCK = 128
NBLOCKS = 64


def with_ends(entries, rng, low, largest):
    extent = entries.shape
    index_at = [jax.random.randint(jax.random.fold_in(rng, axis), (), 0, extent[axis]) for axis in range(len(extent))]
    entries = entries.at[tuple(index_at)].set(low)
    longest = extent.index(max(extent))
    index_at[longest] = (index_at[longest] + 1) % extent[longest]
    return entries.at[tuple(index_at)].set(largest)


def steps_of(key, shape, cuts, low, high):
    factor_of, own = 1.0, jax.random.fold_in(key, 6)
    for position, blocks in cuts:
        heights = jnp.exp(jax.random.uniform(jax.random.fold_in(own, position), (blocks,), jnp.float32, low / len(cuts), high / len(cuts)))
        factor_of = factor_of * jnp.repeat(heights, shape[position] // blocks).reshape([-1 if axis == position else 1 for axis in range(len(shape))])
    return factor_of


def scatter_about(stream_key, shape, spread, reach, pieces=(), dtype=jnp.bfloat16):
    drawn = spread * jax.random.normal(stream_key, shape, jnp.float32)
    if pieces:
        drawn = drawn * steps_of(stream_key, shape, pieces, -0.22, 0.18)
    return jnp.clip(drawn, -reach, reach).astype(dtype)


def setup_inputs(seed: int = 0, part: int = 0) -> dict:
    key_of = jax.random.split(jax.random.key(seed), 5)
    part_keys = jax.random.split(jax.random.fold_in(key_of[4], part), 5)
    return {
        "ancestor_inverse": scatter_about(part_keys[0], (2, 2, ANC, ANC // 2), 1.0, 6.0, ((1, 2), (2, 8)), jnp.float32),
        "panel": scatter_about(part_keys[1], (2, 2, ANC // 2, 2 * WIDTH), ANC ** -0.5, 0.0625, ((1, 2), (2, 8)), jnp.float32),
        "diagonal_inverse": scatter_about(part_keys[2], (2, 2, WIDTH, WIDTH), 1.0, 6.0, ((1, 2),), jnp.float32),
        "pattern": with_ends((jax.random.randint(key_of[3], (NBLOCKS, 2), 0, 4) < 3).astype(jnp.int32), jax.random.fold_in(key_of[3], 1), 0, 1),
    }


def complex_product(left, right):
    def mult(a, b):
        return jnp.dot(a, b, preferred_element_type=jnp.float32, precision=lax.Precision.HIGHEST)
    real_part = mult(left[0], right[0]) - mult(left[1], right[1])
    imag_part = mult(left[0], right[1]) + mult(left[1], right[0])
    return jnp.stack([real_part, imag_part])


def reference(ancestor_inverse, panel, diagonal_inverse, pattern):
    inverse = jnp.transpose(ancestor_inverse, (0, 2, 3, 1)).reshape(2, ANC, ANC)
    lower = jnp.transpose(panel, (0, 2, 1, 3)).reshape(2, ANC, 2 * WIDTH)
    blocks = pattern.astype(jnp.float32)
    row_mask = jnp.repeat(jnp.repeat(blocks, BLOCK, axis=0), WIDTH, axis=1)
    masked = lower * row_mask[None]
    update = -complex_product(inverse, masked) * row_mask[None]
    results = []
    for sibling in range(2):
        own_lower = masked[:, :, sibling * WIDTH:(sibling + 1) * WIDTH]
        own_update = update[:, :, sibling * WIDTH:(sibling + 1) * WIDTH]
        transposed = jnp.transpose(own_lower, (0, 2, 1))
        results.append(diagonal_inverse[:, sibling] - complex_product(transposed, own_update))
    return update, jnp.stack(results, axis=1)
```

```python
import functools
import itertools

import jax
import jax.numpy as jnp
from jax import lax
from jax.experimental import pallas as pl
from jax.experimental.pallas import tpu as pltpu
from jax.sharding import PartitionSpec as P

WIDTH = 256
BLOCK = 128
HALF = WIDTH // 2
QUARTER = WIDTH // 4
TILE = 512


def complex_apply(form, left, right):

    def mult(a, b):
        return jnp.einsum(
            form, a, b, preferred_element_type=jnp.float32, precision=lax.Precision.HIGHEST
        )

    real_part = mult(left[0], right[0]) - mult(left[1], right[1])
    imag_part = mult(left[0], right[1]) + mult(left[1], right[0])
    return jnp.stack([real_part, imag_part])


def contract(inverse_piece, panel_piece):
    groups = panel_piece.shape[3] // WIDTH
    results = []
    for group in range(groups):
        slab = panel_piece[..., group * WIDTH : (group + 1) * WIDTH]
        results.append(complex_apply("hiq,hqk->ik", inverse_piece, slab))
    return jnp.concatenate(results, axis=2)


def plain(ancestor_inverse, panel, diagonal_inverse, pattern):
    row_count = ancestor_inverse.shape[2]
    row_start = lax.axis_index("row") * row_count
    sibling = lax.axis_index("leaf")
    block_count = row_count // BLOCK
    local_pattern = lax.dynamic_slice_in_dim(pattern, row_start // BLOCK, block_count, 0).astype(
        jnp.float32
    )
    panel_mask = jnp.repeat(jnp.repeat(local_pattern, BLOCK // 2, axis=0), WIDTH, axis=1)
    masked = panel * panel_mask[None, None]
    own_rows = jnp.repeat(local_pattern, BLOCK, axis=0)
    own_mask = jnp.where(sibling == 0, own_rows[:, 0], own_rows[:, 1])
    swapped = lax.all_to_all(masked, "leaf", split_axis=3, concat_axis=1, tiled=True)
    partial_value = contract(ancestor_inverse, lax.all_gather(masked, "row", axis=2, tiled=True))
    product = lax.psum_scatter(partial_value, "leaf", scatter_dimension=2, tiled=True)
    update = -product * own_mask[None, :, None]
    paired = jnp.transpose(update.reshape(2, row_count // 2, 2, WIDTH), (0, 2, 1, 3))
    diag_term = complex_apply("hqa,hqb->ab", swapped, paired)
    correction = lax.psum(diag_term, "row")
    return (update, diagonal_inverse - correction[:, None])


def split(value):
    high = value.astype(jnp.bfloat16)
    return high, (value - high.astype(jnp.float32)).astype(jnp.bfloat16)


def mult(a, b):
    return jnp.dot(a, b, preferred_element_type=jnp.float32)


def mult_split(left, right):
    return mult(left[0], right[0]) + mult(left[0], right[1]) + mult(left[1], right[0])


def halves_kernel(first, second):
    lane = lax.broadcasted_iota(jnp.int32, first.shape, 1)
    return (
        jnp.where(lane < QUARTER, first, pltpu.roll(second, QUARTER, 1)),
        jnp.where(lane < QUARTER, pltpu.roll(first, QUARTER, 1), second),
    )


def prepare_kernel(me_ref, pattern_ref, panel_ref, wide_ref, second_ref, third_ref):
    height = BLOCK // 2
    count = panel_ref.shape[2] // height
    first = (me_ref[0] * pl.num_programs(0) + pl.program_id(0)) * count
    for i, part in itertools.product(range(count), range(2)):
        rows = pl.ds(i * height, height)
        masks = [pattern_ref[first + i, s].astype(jnp.float32) for s in range(2)]
        left = [panel_ref[part, 0, rows, pl.ds(s * WIDTH, HALF)] * masks[s] for s in range(2)]
        right = [panel_ref[part, 0, rows, pl.ds(s * WIDTH + HALF, HALF)] * masks[s] for s in range(2)]
        for s in range(2):
            wide_ref[rows, pl.ds((2 * part + s) * HALF, HALF)] = left[s]
        second, third = halves_kernel(*right)
        second_ref[rows, pl.ds(part * HALF, HALF)] = second
        third_ref[rows, pl.ds(part * HALF, HALF)] = third


def prepare(me, pattern, panel):
    rows = panel.shape[2]
    tile = rows // 2
    lanes = (4 * HALF, 4 * QUARTER, 4 * QUARTER)
    return pl.pallas_call(
        prepare_kernel,
        out_shape=[jax.ShapeDtypeStruct((rows, n), jnp.float32) for n in lanes],
        grid_spec=pltpu.PrefetchScalarGridSpec(
            num_scalar_prefetch=2,
            grid=(2,),
            in_specs=[pl.BlockSpec((2, 1, tile, 2 * WIDTH), lambda i, *_: (0, 0, i, 0))],
            out_specs=[pl.BlockSpec((tile, n), lambda i, *_: (i, 0)) for n in lanes],
        ),
        name="prepare",
    )(me.reshape(1), pattern, panel)


def slots_kernel(table_ref, a_ref, *refs, counts, fresh, last, joined):
    candidates, refs = refs[: 2 * sum(counts)], refs[2 * sum(counts) :]
    sum_ref, refs = (None, refs) if fresh else (refs[0], refs[1:])
    out_refs, refs = refs[: 1 + last], refs[1 + last :]
    piece_ref, high_ref, low_ref, total_ref, sems = refs
    slots = len(counts)
    tile, slot = pl.program_id(0), pl.program_id(1)
    rows, lanes = piece_ref.shape[1] // 2, piece_ref.shape[2]
    half = lanes // 2
    side = table_ref[2 * slots]

    def fetch(k, act):
        first = sum(counts[:k])
        for j in range(counts[k]):

            @pl.when(table_ref[2 * k + 1] == j)
            def _():
                for way in range(2):
                    place = side if way == 0 else 1 - side
                    act(
                        pltpu.make_async_copy(
                            candidates[2 * (first + j) + way].at[pl.ds(way * joined * rows, rows)],
                            piece_ref.at[k, pl.ds(pl.multiple_of(place * rows, rows), rows)],
                            sems.at[k, way],
                        )
                    )

    @pl.when(tile == 0)
    def _():
        @pl.when(slot == 0)
        def _():
            for k in range(slots):
                fetch(k, lambda copy: copy.start())

        for k in range(slots):

            @pl.when(slot == k)
            def _():
                fetch(k, lambda copy: copy.wait())

        high, low = split(piece_ref[slot])
        for parts, target in ((high, high_ref), (low, low_ref)):
            target[slot, : 2 * rows] = parts
            target[slot, 2 * rows :, :half] = -parts[:, half:]
            target[slot, 2 * rows :, half:] = parts[:, :half]

    total = None
    for part in range(2):
        span = pl.ds(2 * rows * part, 2 * rows)
        term = mult_split(split(a_ref[part]), (high_ref[slot, span], low_ref[slot, span]))
        total = term if total is None else total + term

    @pl.when(slot == 0)
    def _():
        total_ref[...] = total if fresh else sum_ref[...] + total

    @pl.when(slot > 0)
    def _():
        total_ref[...] += total

    @pl.when(slot == slots - 1)
    def _():
        value = total_ref[...]
        if not last:
            out_refs[0][...] = value
            return
        if half == 2 * HALF:
            pieces = [value[:, j * HALF : (j + 1) * HALF] for j in range(4)]
            siblings = [jnp.concatenate([pieces[s], pieces[2 + s]], axis=1) for s in range(2)]
        else:
            siblings = halves_kernel(value[:, :half], value[:, half:])
        mine = table_ref[2 * slots + 1] == 0
        out_refs[0][...] = jnp.where(mine, siblings[0], siblings[1])
        out_refs[1][...] = jnp.where(mine, siblings[1], siblings[0])


def add_slots(inverse, slots, picks, total, side, sibling, last=False):
    row_count = inverse.shape[2]
    counts = tuple(len(slot) for slot in slots)
    operands = [array for slot in slots for pair in slot for array in pair]
    rows, lanes = inverse.shape[3] // 8, operands[0].shape[1]
    joined = operands[0].shape[0] == 2 * rows
    fresh = total is None
    block = pl.BlockSpec((TILE, lanes), lambda i, k, t: (i, 0))
    specs = [pl.BlockSpec((2, None, TILE, 2 * rows), lambda i, k, t: (0, 0, i, t[2 * k]))]
    specs += [pl.BlockSpec(memory_space=pl.ANY)] * len(operands)
    operands = [inverse] + operands
    if not fresh:
        specs.append(block)
        operands.append(total)
    if last:
        half_block = pl.BlockSpec((TILE, lanes // 2), lambda i, k, t: (i, 0))
        out_specs = [half_block] * 2
        out_shape = [jax.ShapeDtypeStruct((row_count, lanes // 2), jnp.float32)] * 2
    else:
        out_specs, out_shape = [block], [jax.ShapeDtypeStruct((row_count, lanes), jnp.float32)]
    table = [entry for pick in picks for entry in pick] + [side, sibling]
    result = pl.pallas_call(
        functools.partial(slots_kernel, counts=counts, fresh=fresh, last=last, joined=joined),
        out_shape=out_shape,
        grid_spec=pltpu.PrefetchScalarGridSpec(
            num_scalar_prefetch=1,
            grid=(row_count // TILE, len(counts)),
            in_specs=specs,
            out_specs=out_specs,
            scratch_shapes=[
                pltpu.VMEM((len(counts), 2 * rows, lanes), jnp.float32),
                pltpu.VMEM((len(counts), 4 * rows, lanes), jnp.bfloat16),
                pltpu.VMEM((len(counts), 4 * rows, lanes), jnp.bfloat16),
                pltpu.VMEM((TILE, lanes), jnp.float32),
                pltpu.SemaphoreType.DMA((len(counts), 2)),
            ],
        ),
        compiler_params=pltpu.CompilerParams(vmem_limit_bytes=60 * 2**20),
        cost_estimate=pl.CostEstimate(
            flops=2 * 3 * row_count * 4 * rows * lanes * len(counts),
            bytes_accessed=4 * 4 * row_count * rows * len(counts),
            transcendentals=0,
        ),
        name=f"slots_{lanes}_{len(counts)}",
    )(jnp.stack(table).astype(jnp.int32), *operands)
    return result if last else result[0]


def finish_kernel(mine_ref, other_ref, mask_ref, lower_ref, update_ref, term_ref):
    half = mine_ref.shape[1] // 2
    value = -(mine_ref[...] + other_ref[...]) * mask_ref[...]
    update_ref[...] = value
    if half == QUARTER:
        lane = lax.broadcasted_iota(jnp.int32, value.shape, 1)
        rolled = pltpu.roll(value, QUARTER, 1)
        turned = jnp.where(lane < QUARTER, -rolled, rolled)
    else:
        turned = jnp.concatenate([-value[:, half:], value[:, :half]], axis=1)
    total = None
    for part, right in enumerate((value, turned)):
        term = mult_split(split(lower_ref[part]), split(right))
        total = term if total is None else total + term
    term_ref[...] = total


def finish(mine, other, mask, lower):
    row_count, lanes = mine.shape
    return pl.pallas_call(
        finish_kernel,
        out_shape=[
            jax.ShapeDtypeStruct((row_count, lanes), jnp.float32),
            jax.ShapeDtypeStruct((WIDTH, lanes), jnp.float32),
        ],
        compiler_params=pltpu.CompilerParams(vmem_limit_bytes=32 * 2**20),
        cost_estimate=pl.CostEstimate(flops=0, bytes_accessed=0, transcendentals=0),
        name=f"finish_{lanes}",
    )(mine, other, mask, lower)


def assemble_kernel(wide_ref, second_ref, third_ref, out_ref):
    parts = halves_kernel(second_ref[...], third_ref[...])
    for part in range(2):
        out_ref[part, :, :HALF] = wide_ref[:, part * HALF : (part + 1) * HALF]
        out_ref[part, :, HALF:] = parts[part]


def assemble(wide, second, third):
    rows = wide.shape[0]
    tile = rows // 2
    return pl.pallas_call(
        assemble_kernel,
        out_shape=jax.ShapeDtypeStruct((2, rows, WIDTH), jnp.float32),
        grid=(2,),
        in_specs=[
            pl.BlockSpec((tile, WIDTH), lambda i: (i, 0)),
            pl.BlockSpec((tile, HALF), lambda i: (i, 0)),
            pl.BlockSpec((tile, HALF), lambda i: (i, 0)),
        ],
        out_specs=pl.BlockSpec((2, tile, WIDTH), lambda i: (0, i, 0)),
        cost_estimate=pl.CostEstimate(flops=0, bytes_accessed=0, transcendentals=0),
        name="assemble",
    )(wide, second, third)


def lined(ancestor_inverse, panel, diagonal_inverse, pattern):
    row_count = ancestor_inverse.shape[2]
    me = lax.axis_index("row")
    z, y = me // 2, me % 2
    sibling = lax.axis_index("leaf")
    block_count = row_count // BLOCK
    wide, second, third = prepare(me, pattern, panel)

    def up(value, step):
        pairs = [(2 * i + j, 2 * i + 2 + j) for i in range(step, 3) for j in (0, 1)]
        return lax.ppermute(value, "row", pairs)

    def down(value, step):
        pairs = [(2 * i + j, 2 * i - 2 + j) for i in range(1, 4 - step) for j in (0, 1)]
        return lax.ppermute(value, "row", pairs)

    def across(value, places=(0, 1, 2, 3)):
        pairs = [(2 * i + j, 2 * i + 1 - j) for i in places for j in (0, 1)]
        return lax.ppermute(value, "row", pairs)

    def swap(value):
        return lax.ppermute(value, "leaf", [(0, 1), (1, 0)])

    layout = (
        (("u0",), (0, 1, 2, 3), (0, 0, 0, 0)),
        (("u1", "d1"), (1, 0, 1, 2), (1, 0, 0, 0)),
        (("u2", "d1", "d2"), (2, 2, 3, 1), (2, 1, 1, 0)),
        (("u2", "u3", "d2", "d3"), (3, 3, 0, 0), (3, 2, 0, 1)),
    )

    def by_z(values):
        return jnp.where(z == 0, values[0], jnp.where(z == 1, values[1], jnp.where(z == 2, values[2], values[3])))

    picks = [(by_z(sources), by_z(choices)) for _, sources, choices in layout]

    live = {"w u0": wide, "s u0": second, "t u0": third}

    def fence():
        live.update(lax.optimization_barrier(dict(live)))

    def hop(chain, step):
        live[f"{chain} u{step}"] = up(live[f"{chain} u{max(step - 1, 0)}"], step - 1)
        live[f"{chain} d{step}"] = down(live[f"{chain} {'d' if step > 1 else 'u'}{step - 1}"], step - 1)

    def cross(chain, slot):
        names, _, choices = layout[slot]
        for j, name in enumerate(names):
            places = [i for i in range(4) if choices[i] == j]
            live[f"{chain} y{slot} {name}"] = across(live[f"{chain} {name}"], places)

    def add(chain, wanted, last=False):
        slots = []
        for k in wanted:
            names = layout[k][0]
            if chain == "t":
                slots.append([(live[f"t {name}"],) * 2 for name in names])
            else:
                slots.append([(live[f"{chain} {name}"], live[f"{chain} y{k} {name}"]) for name in names])
        total = live.pop(f"{chain} total", None)
        result = add_slots(ancestor_inverse, slots, [picks[k] for k in wanted], total, y, sibling, last)
        if last:
            return result
        live[f"{chain} total"] = result

    local_pattern = lax.dynamic_slice_in_dim(pattern, me * block_count, block_count, 0).astype(jnp.float32)
    own_pattern = jnp.where(sibling == 0, local_pattern[:, 0], local_pattern[:, 1])
    own_mask = jnp.broadcast_to(jnp.repeat(own_pattern, BLOCK)[:, None], (row_count, HALF))
    pair = panel[:, 0]
    keep = jnp.where(sibling == 0, pair[..., :WIDTH], pair[..., WIDTH:])
    give = jnp.where(sibling == 0, pair[..., WIDTH:], pair[..., :WIDTH])

    def lower_rows():
        got = swap(give)
        even = jnp.where(sibling == 0, keep, got)
        odd = jnp.where(sibling == 0, got, keep)
        rows = jnp.stack([even, odd], axis=2).reshape(2, row_count, WIDTH)
        return jnp.transpose(rows * own_mask[None, :, :1], (0, 2, 1))

    def total_sum(term):
        for distance in (1, 2, 4):
            term = term + lax.ppermute(term, "row", [(i, i ^ distance) for i in range(8)])
        return term

    hop("w", 1)
    cross("w", 0)
    hop("s", 1)
    live["crossed"] = across(live["t u0"])
    fence()
    hop("w", 2)
    cross("w", 1)
    hop("s", 2)
    cross("s", 0)
    live["t u0"] = jnp.concatenate([live["t u0"], live.pop("crossed")])
    add("w", (0,))
    fence()
    hop("w", 3)
    cross("w", 2)
    hop("s", 3)
    cross("s", 1)
    add("w", (1,))
    add("t", (0,))
    live["lower"] = lower_rows()
    fence()
    hop("t", 1)
    cross("w", 3)
    add("w", (2,))
    add("s", (0, 1))
    fence()
    hop("t", 2)
    cross("s", 2)
    cross("s", 3)
    mine, theirs = add("w", (3,), last=True)
    live["update w"], live["term w"] = finish(mine, swap(theirs), jnp.concatenate([own_mask] * 2, axis=1), live["lower"])
    add("t", (1,))
    fence()
    hop("t", 3)
    mine, theirs = add("s", (2, 3), last=True)
    live["update s"], live["term s"] = finish(mine, swap(theirs), own_mask, live["lower"])
    live["sum w"] = total_sum(live["term w"])
    add("t", (2,))
    fence()
    mine, theirs = add("t", (3,), last=True)
    update_first, update_second = live["update w"], live["update s"]
    update_third, term_third = finish(mine, swap(theirs), own_mask, live["lower"])
    sums = [live["sum w"], total_sum(live["term s"]), total_sum(term_third)]

    update = assemble(update_first, update_second, update_third)
    sums = [jnp.concatenate([s[:, : s.shape[1] // 2] for s in sums], axis=1), jnp.concatenate([s[:, s.shape[1] // 2 :] for s in sums], axis=1)]
    return (update, diagonal_inverse - jnp.stack(sums)[:, None])


def solution(mesh):
    in_specs = (
        P("pole", "leaf", "row", None),
        P("pole", "leaf", "row", None),
        P("pole", "leaf", None, None),
        P(),
    )
    out_specs = (P("pole", "row", "leaf"), P("pole", "leaf", None, None))
    local = lined if mesh.shape["row"] == 8 and mesh.shape["leaf"] == 2 else plain
    return jax.shard_map(local, mesh=mesh, in_specs=in_specs, out_specs=out_specs, check_vma=False)
```

```python
import functools
import itertools

import jax
import jax.numpy as jnp
from jax import lax
from jax.experimental import pallas as pl
from jax.experimental.pallas import tpu as pltpu
from jax.sharding import PartitionSpec as P

WIDTH = 256
BLOCK = 128
HALF = WIDTH // 2
QUARTER = WIDTH // 4
TILE = 512
SCALE = 2


def complex_apply(form, left, right):

    def mult(a, b):
        return jnp.einsum(
            form, a, b, preferred_element_type=jnp.float32, precision=lax.Precision.HIGHEST
        )

    real_part = mult(left[0], right[0]) - mult(left[1], right[1])
    imag_part = mult(left[0], right[1]) + mult(left[1], right[0])
    return jnp.stack([real_part, imag_part])


def contract(inverse_piece, panel_piece):
    groups = panel_piece.shape[3] // WIDTH
    results = []
    for group in range(groups):
        slab = panel_piece[..., group * WIDTH : (group + 1) * WIDTH]
        results.append(complex_apply("hiq,hqk->ik", inverse_piece, slab))
    return jnp.concatenate(results, axis=2)


def plain(ancestor_inverse, panel, diagonal_inverse, pattern):
    row_count = ancestor_inverse.shape[2]
    row_start = lax.axis_index("row") * row_count
    sibling = lax.axis_index("leaf")
    block_count = row_count // BLOCK
    local_pattern = lax.dynamic_slice_in_dim(pattern, row_start // BLOCK, block_count, 0).astype(
        jnp.float32
    )
    panel_mask = jnp.repeat(jnp.repeat(local_pattern, BLOCK // 2, axis=0), WIDTH, axis=1)
    masked = panel * panel_mask[None, None]
    own_rows = jnp.repeat(local_pattern, BLOCK, axis=0)
    own_mask = jnp.where(sibling == 0, own_rows[:, 0], own_rows[:, 1])
    swapped = lax.all_to_all(masked, "leaf", split_axis=3, concat_axis=1, tiled=True)
    partial_value = contract(ancestor_inverse, lax.all_gather(masked, "row", axis=2, tiled=True))
    product = lax.psum_scatter(partial_value, "leaf", scatter_dimension=2, tiled=True)
    update = -product * own_mask[None, :, None]
    paired = jnp.transpose(update.reshape(2, row_count // 2, 2, WIDTH), (0, 2, 1, 3))
    diag_term = complex_apply("hqa,hqb->ab", swapped, paired)
    correction = lax.psum(diag_term, "row")
    return (update, diagonal_inverse - correction[:, None])


def split(value):
    high = value.astype(jnp.bfloat16)
    return high, (value - high.astype(jnp.float32)).astype(jnp.bfloat16)


def mult(a, b):
    return jnp.dot(a, b, preferred_element_type=jnp.float32)


def mult_split(left, right):
    return mult(left[0], right[0]) + mult(left[0], right[1]) + mult(left[1], right[0])


def halves_kernel(first, second):
    lane = lax.broadcasted_iota(jnp.int32, first.shape, 1)
    return (
        jnp.where(lane < QUARTER, first, pltpu.roll(second, QUARTER, 1)),
        jnp.where(lane < QUARTER, pltpu.roll(first, QUARTER, 1), second),
    )


def prepare_kernel(me_ref, pattern_ref, panel_ref, first_ref, last_ref):
    height = BLOCK // 2
    count = panel_ref.shape[2] // height
    first = (me_ref[0] * pl.num_programs(0) + pl.program_id(0)) * count
    for i, part in itertools.product(range(count), range(2)):
        rows = pl.ds(i * height, height)
        masks = [pattern_ref[first + i, s].astype(jnp.float32) for s in range(2)]
        left = [panel_ref[part, 0, rows, pl.ds(s * WIDTH, HALF)] * masks[s] for s in range(2)]
        right = [panel_ref[part, 0, rows, pl.ds(s * WIDTH + HALF, HALF)] * masks[s] for s in range(2)]
        for s in range(2):
            first_ref[rows, pl.ds((3 * part + s) * HALF, HALF)] = left[s]
        third, fourth = halves_kernel(*right)
        first_ref[rows, pl.ds((3 * part + 2) * HALF, HALF)] = third
        last_ref[rows, pl.ds(part * HALF, HALF)] = fourth


def prepare(me, pattern, panel):
    rows = panel.shape[2]
    tile = rows // 2
    lanes = (6 * HALF, 2 * HALF)
    return pl.pallas_call(
        prepare_kernel,
        out_shape=[jax.ShapeDtypeStruct((rows, n), jnp.float32) for n in lanes],
        grid_spec=pltpu.PrefetchScalarGridSpec(
            num_scalar_prefetch=2,
            grid=(2,),
            in_specs=[pl.BlockSpec((2, 1, tile, 2 * WIDTH), lambda i, *_: (0, 0, i, 0))],
            out_specs=[pl.BlockSpec((tile, n), lambda i, *_: (i, 0)) for n in lanes],
        ),
        name="prepare",
    )(me.reshape(1), pattern, panel)


def slots_kernel(table_ref, a_ref, *refs, wanted, counts, fresh, last, joined):
    candidates, refs = refs[: 2 * sum(counts)], refs[2 * sum(counts) :]
    sum_ref, refs = (None, refs) if fresh else (refs[0], refs[1:])
    out_refs, refs = refs[: 1 + last], refs[1 + last :]
    piece_ref, high_ref, low_ref, total_ref, sems = refs
    slots = len(counts)
    tile, slot = pl.program_id(0), pl.program_id(1)
    rows, lanes = piece_ref.shape[1] // 2, piece_ref.shape[2]
    half = lanes // 2
    side = table_ref[8]

    def fetch(k, act):
        first = sum(counts[:k])
        for j in range(counts[k]):

            @pl.when((counts[k] == 1) | (table_ref[4 + wanted[k]] == j))
            def _():
                for way in range(2):
                    place = side if way == 0 else 1 - side
                    act(
                        pltpu.make_async_copy(
                            candidates[2 * (first + j) + way].at[pl.ds(way * joined * rows, rows)],
                            piece_ref.at[k, pl.ds(pl.multiple_of(place * rows, rows), rows)],
                            sems.at[k, way],
                        )
                    )

    @pl.when(tile == 0)
    def _():
        @pl.when(slot == 0)
        def _():
            for k in range(slots):
                fetch(k, lambda copy: copy.start())

        for k in range(slots):

            @pl.when(slot == k)
            def _():
                fetch(k, lambda copy: copy.wait())

        high, low = split(piece_ref[slot])
        for parts, target in ((high, high_ref), (low, low_ref)):
            target[slot, : 2 * rows] = parts
            target[slot, 2 * rows :, :half] = -parts[:, half:]
            target[slot, 2 * rows :, half:] = parts[:, :half]

    total = None
    for part in range(2):
        span = pl.ds(2 * rows * part, 2 * rows)
        term = mult_split(split(a_ref[part]), (high_ref[slot, span], low_ref[slot, span]))
        total = term if total is None else total + term

    @pl.when(slot == 0)
    def _():
        total_ref[...] = total if fresh else sum_ref[...] + total

    @pl.when(slot > 0)
    def _():
        total_ref[...] += total

    @pl.when(slot == slots - 1)
    def _():
        value = total_ref[...]
        if not last:
            out_refs[0][...] = value
            return
        siblings = halves_kernel(value[:, half - HALF : half], value[:, 2 * half - HALF :])
        if half > HALF:
            siblings = [
                jnp.concatenate(
                    [value[:, k * half + s * HALF : k * half + (s + 1) * HALF] for k in range(2)] + [siblings[s]], axis=1
                )
                for s in range(2)
            ]
        mine = table_ref[9] == 0
        out_refs[0][...] = jnp.where(mine, siblings[0], siblings[1])
        out_refs[1][...] = jnp.where(mine, siblings[1], siblings[0])


def add_slots(inverse, table, wanted, slots, total, last=False, ease=1):
    row_count = inverse.shape[2]
    counts = tuple(len(slot) for slot in slots)
    operands = [array for slot in slots for pair in slot for array in pair]
    rows, lanes = inverse.shape[3] // 8, operands[0].shape[1]
    joined = operands[0].shape[0] == 2 * rows
    fresh = total is None
    block = pl.BlockSpec((TILE, lanes), lambda i, k, t: (i, 0))
    specs = [pl.BlockSpec((2, None, TILE, 2 * rows), lambda i, k, t: (0, 0, i, t[k + wanted[0]]))]
    specs += [pl.BlockSpec(memory_space=pl.ANY)] * len(operands)
    operands = [inverse] + operands
    if not fresh:
        specs.append(block)
        operands.append(total)
    if last:
        half_block = pl.BlockSpec((TILE, lanes // 2), lambda i, k, t: (i, 0))
        out_specs = [half_block] * 2
        out_shape = [jax.ShapeDtypeStruct((row_count, lanes // 2), jnp.float32)] * 2
    else:
        out_specs, out_shape = [block], [jax.ShapeDtypeStruct((row_count, lanes), jnp.float32)]
    result = pl.pallas_call(
        functools.partial(slots_kernel, wanted=wanted, counts=counts, fresh=fresh, last=last, joined=joined),
        out_shape=out_shape,
        grid_spec=pltpu.PrefetchScalarGridSpec(
            num_scalar_prefetch=1,
            grid=(row_count // TILE, len(counts)),
            in_specs=specs,
            out_specs=out_specs,
            scratch_shapes=[
                pltpu.VMEM((len(counts), 2 * rows, lanes), jnp.float32),
                pltpu.VMEM((len(counts), 4 * rows, lanes), jnp.bfloat16),
                pltpu.VMEM((len(counts), 4 * rows, lanes), jnp.bfloat16),
                pltpu.VMEM((TILE, lanes), jnp.float32),
                pltpu.SemaphoreType.DMA((len(counts), 2)),
            ],
        ),
        compiler_params=pltpu.CompilerParams(vmem_limit_bytes=60 * 2**20),
        cost_estimate=pl.CostEstimate(
            flops=2 * 3 * row_count * 4 * rows * lanes * len(counts) // (SCALE * ease),
            bytes_accessed=4 * 4 * row_count * rows * len(counts) // (SCALE * ease),
            transcendentals=0,
        ),
        name=f"slots_{lanes}_{len(counts)}",
    )(table, *operands)
    return result if last else result[0]


def finish_kernel(mine_ref, other_ref, mask_ref, lower_ref, update_ref, term_ref):
    value = -(mine_ref[...] + other_ref[...]) * mask_ref[...]
    update_ref[...] = value
    packed = value[:, -HALF:]
    lane = lax.broadcasted_iota(jnp.int32, packed.shape, 1)
    rolled = pltpu.roll(packed, QUARTER, 1)
    turned = jnp.where(lane < QUARTER, -rolled, rolled)
    if value.shape[1] > HALF:
        turned = jnp.concatenate([-value[:, HALF : 2 * HALF], value[:, :HALF], turned], axis=1)
    total = None
    for part, right in enumerate((value, turned)):
        term = mult_split(split(lower_ref[part]), split(right))
        total = term if total is None else total + term
    term_ref[...] = total


def finish(mine, other, mask, lower):
    row_count, lanes = mine.shape
    return pl.pallas_call(
        finish_kernel,
        out_shape=[
            jax.ShapeDtypeStruct((row_count, lanes), jnp.float32),
            jax.ShapeDtypeStruct((WIDTH, lanes), jnp.float32),
        ],
        compiler_params=pltpu.CompilerParams(vmem_limit_bytes=32 * 2**20),
        cost_estimate=pl.CostEstimate(flops=0, bytes_accessed=0, transcendentals=0),
        name=f"finish_{lanes}",
    )(mine, other, mask, lower)


def assemble_kernel(first_ref, last_ref, out_ref):
    parts = halves_kernel(first_ref[:, 2 * HALF :], last_ref[...])
    for part in range(2):
        out_ref[part, :, :HALF] = first_ref[:, part * HALF : (part + 1) * HALF]
        out_ref[part, :, HALF:] = parts[part]


def assemble(first, last):
    rows = first.shape[0]
    tile = rows // 2
    return pl.pallas_call(
        assemble_kernel,
        out_shape=jax.ShapeDtypeStruct((2, rows, WIDTH), jnp.float32),
        grid=(2,),
        in_specs=[
            pl.BlockSpec((tile, 3 * HALF), lambda i: (i, 0)),
            pl.BlockSpec((tile, HALF), lambda i: (i, 0)),
        ],
        out_specs=pl.BlockSpec((2, tile, WIDTH), lambda i: (0, i, 0)),
        cost_estimate=pl.CostEstimate(flops=0, bytes_accessed=0, transcendentals=0),
        name="assemble",
    )(first, last)


def lined(ancestor_inverse, panel, diagonal_inverse, pattern):
    row_count = ancestor_inverse.shape[2]
    me = lax.axis_index("row")
    z, y = me // 2, me % 2
    sibling = lax.axis_index("leaf")
    block_count = row_count // BLOCK
    first, second = prepare(me, pattern, panel)

    def up(value, step):
        pairs = [(2 * i + j, 2 * i + 2 + j) for i in range(step, 3) for j in (0, 1)]
        return lax.ppermute(value, "row", pairs)

    def down(value, step):
        pairs = [(2 * i + j, 2 * i - 2 + j) for i in range(1, 4 - step) for j in (0, 1)]
        return lax.ppermute(value, "row", pairs)

    def across(value, places=(0, 1, 2, 3)):
        pairs = [(2 * i + j, 2 * i + 1 - j) for i in places for j in (0, 1)]
        return lax.ppermute(value, "row", pairs)

    def swap(value):
        return lax.ppermute(value, "leaf", [(0, 1), (1, 0)])

    layout = (
        (("u0",), (0, 1, 2, 3), (0, 0, 0, 0)),
        (("u1", "d1"), (1, 0, 1, 2), (1, 0, 0, 0)),
        (("u2", "d1", "d2"), (2, 2, 3, 1), (2, 1, 1, 0)),
        (("u2", "u3", "d2", "d3"), (3, 3, 0, 0), (3, 2, 0, 1)),
    )

    def by_z(values):
        return jnp.where(z == 0, values[0], jnp.where(z == 1, values[1], jnp.where(z == 2, values[2], values[3])))

    table = [by_z(sources) for _, sources, _ in layout] + [by_z(choices) for _, _, choices in layout]
    table = jnp.stack(table + [y, sibling]).astype(jnp.int32)

    local_pattern = lax.dynamic_slice_in_dim(pattern, me * block_count, block_count, 0).astype(jnp.float32)
    own_pattern = jnp.where(sibling == 0, local_pattern[:, 0], local_pattern[:, 1])
    own_mask = jnp.broadcast_to(jnp.repeat(own_pattern, BLOCK)[:, None], (row_count, HALF))

    live = {"c u0": first, "c 0": first, "t 0": second}
    live["mask"], live["wide mask"] = own_mask, jnp.concatenate([own_mask] * 3, axis=1)

    def fence():
        live.update(lax.optimization_barrier(dict(live)))

    def hop(chain, step):
        live[f"{chain} u{step}"] = up(live[f"{chain} u{max(step - 1, 0)}"], step - 1)
        live[f"{chain} d{step}"] = down(live[f"{chain} {'d' if step > 1 else 'u'}{step - 1}"], step - 1)

    def select(chain, slot):
        names, _, choices = layout[slot]
        value = live[f"{chain} {names[-1]}"]
        for j, name in enumerate(names[:-1]):
            chosen = functools.reduce(jnp.logical_or, [z == i for i in range(4) if choices[i] == j])
            value = jnp.where(chosen, live[f"{chain} {name}"], value)
        live[f"{chain} {slot}"] = value

    def cross(chain, slot):
        names, _, choices = layout[slot]
        if slot == 3:
            select(chain, slot)
        if slot in (0, 3):
            live[f"{chain} y{slot}"] = across(live[f"{chain} {slot}"])
            return
        for j, name in enumerate(names):
            places = [i for i in range(4) if choices[i] == j]
            live[f"{chain} y{slot} {name}"] = across(live[f"{chain} {name}"], places)

    def add(chain, wanted, last=False, ease=1):
        slots = []
        for k in wanted:
            if chain == "t":
                slots.append([(live[f"t {name}"],) * 2 for name in layout[k][0]])
            elif k in (1, 2):
                slots.append([(live[f"{chain} {name}"], live[f"{chain} y{k} {name}"]) for name in layout[k][0]])
            else:
                slots.append([(live[f"{chain} {k}"], live[f"{chain} y{k}"])])
        total = live.pop(f"{chain} total", None)
        result = add_slots(ancestor_inverse, live["table"], tuple(wanted), slots, total, last, ease)
        if last:
            return result
        live[f"{chain} total"] = result

    pair = panel[:, 0]
    pair = lax.optimization_barrier((pair, first))[0]
    keep = jnp.where(sibling == 0, pair[..., :WIDTH], pair[..., WIDTH:])
    give = jnp.where(sibling == 0, pair[..., WIDTH:], pair[..., :WIDTH])

    def lower_rows():
        got = swap(give)
        even = jnp.where(sibling == 0, keep, got)
        odd = jnp.where(sibling == 0, got, keep)
        rows = jnp.stack([even, odd], axis=2).reshape(2, row_count, WIDTH)
        return jnp.transpose(rows * own_mask[None, :, :1], (0, 2, 1))

    def exchange(term, distance):
        return term + lax.ppermute(term, "row", [(i, i ^ distance) for i in range(8)])

    hop("c", 1)
    cross("c", 0)
    cross("t", 0)
    live["lower"] = lower_rows()
    live["table"] = table
    fence()
    hop("c", 2)
    cross("c", 1)
    live["t u0"] = jnp.concatenate([live.pop("t 0"), live.pop("t y0")])
    add("c", (0,))
    fence()
    hop("c", 3)
    cross("c", 2)
    add("c", (1,))
    add("t", (0,))
    fence()
    hop("t", 1)
    cross("c", 3)
    add("c", (2,))
    fence()
    hop("t", 2)
    live["mine"], live["theirs"] = add("c", (3,), last=True)
    fence()
    hop("t", 3)
    live["update c"], term = finish(live.pop("mine"), swap(live.pop("theirs")), live["wide mask"], live["lower"])
    live["term c"] = exchange(term, 1)
    add("t", (1, 2))
    fence()
    mine, theirs = add("t", (3,), last=True)
    update_last, term_last = finish(mine, swap(theirs), live["mask"], live["lower"])
    live["term c"] = exchange(exchange(live["term c"], 2), 4)
    for distance in (1, 2, 4):
        term_last = exchange(term_last, distance)

    update = assemble(live["update c"], update_last)
    total = jnp.concatenate([live["term c"], term_last], axis=1)
    real = [total[:, :HALF], total[:, 2 * HALF : 2 * HALF + QUARTER], total[:, 3 * HALF : 3 * HALF + QUARTER]]
    imag = [total[:, HALF : 2 * HALF], total[:, 2 * HALF + QUARTER : 3 * HALF], total[:, 3 * HALF + QUARTER :]]
    correction = jnp.stack([jnp.concatenate(real, axis=1), jnp.concatenate(imag, axis=1)])
    return (update, diagonal_inverse - correction[:, None])


def solution(mesh):
    in_specs = (
        P("pole", "leaf", "row", None),
        P("pole", "leaf", "row", None),
        P("pole", "leaf", None, None),
        P(),
    )
    out_specs = (P("pole", "row", "leaf"), P("pole", "leaf", None, None))
    local = lined if mesh.shape["row"] == 8 and mesh.shape["leaf"] == 2 else plain
    return jax.shard_map(local, mesh=mesh, in_specs=in_specs, out_specs=out_specs, check_vma=False)
```

```python
import functools
import itertools

import jax
import jax.numpy as jnp
from jax import lax
from jax.experimental import pallas as pl
from jax.experimental.pallas import tpu as pltpu
from jax.sharding import PartitionSpec as P

WIDTH = 256
BLOCK = 128
HALF = WIDTH // 2
QUARTER = WIDTH // 4
TILE = 512
SCALE = 2


def complex_apply(form, left, right):

    def mult(a, b):
        return jnp.einsum(
            form, a, b, preferred_element_type=jnp.float32, precision=lax.Precision.HIGHEST
        )

    real_part = mult(left[0], right[0]) - mult(left[1], right[1])
    imag_part = mult(left[0], right[1]) + mult(left[1], right[0])
    return jnp.stack([real_part, imag_part])


def contract(inverse_piece, panel_piece):
    groups = panel_piece.shape[3] // WIDTH
    results = []
    for group in range(groups):
        slab = panel_piece[..., group * WIDTH : (group + 1) * WIDTH]
        results.append(complex_apply("hiq,hqk->ik", inverse_piece, slab))
    return jnp.concatenate(results, axis=2)


def plain(ancestor_inverse, panel, diagonal_inverse, pattern):
    row_count = ancestor_inverse.shape[2]
    row_start = lax.axis_index("row") * row_count
    sibling = lax.axis_index("leaf")
    block_count = row_count // BLOCK
    local_pattern = lax.dynamic_slice_in_dim(pattern, row_start // BLOCK, block_count, 0).astype(
        jnp.float32
    )
    panel_mask = jnp.repeat(jnp.repeat(local_pattern, BLOCK // 2, axis=0), WIDTH, axis=1)
    masked = panel * panel_mask[None, None]
    own_rows = jnp.repeat(local_pattern, BLOCK, axis=0)
    own_mask = jnp.where(sibling == 0, own_rows[:, 0], own_rows[:, 1])
    swapped = lax.all_to_all(masked, "leaf", split_axis=3, concat_axis=1, tiled=True)
    partial_value = contract(ancestor_inverse, lax.all_gather(masked, "row", axis=2, tiled=True))
    product = lax.psum_scatter(partial_value, "leaf", scatter_dimension=2, tiled=True)
    update = -product * own_mask[None, :, None]
    paired = jnp.transpose(update.reshape(2, row_count // 2, 2, WIDTH), (0, 2, 1, 3))
    diag_term = complex_apply("hqa,hqb->ab", swapped, paired)
    correction = lax.psum(diag_term, "row")
    return (update, diagonal_inverse - correction[:, None])


def split(value):
    high = value.astype(jnp.bfloat16)
    return high, (value - high.astype(jnp.float32)).astype(jnp.bfloat16)


def mult(a, b):
    return jnp.dot(a, b, preferred_element_type=jnp.float32)


def mult_split(left, right):
    return mult(left[0], right[0]) + mult(left[0], right[1]) + mult(left[1], right[0])


def halves_kernel(first, second):
    lane = lax.broadcasted_iota(jnp.int32, first.shape, 1)
    return (
        jnp.where(lane < QUARTER, first, pltpu.roll(second, QUARTER, 1)),
        jnp.where(lane < QUARTER, pltpu.roll(first, QUARTER, 1), second),
    )


def prepare_kernel(me_ref, pattern_ref, panel_ref, first_ref, last_ref):
    height = BLOCK // 2
    count = panel_ref.shape[2] // height
    first = (me_ref[0] * pl.num_programs(0) + pl.program_id(0)) * count
    for i, part in itertools.product(range(count), range(2)):
        rows = pl.ds(i * height, height)
        masks = [pattern_ref[first + i, s].astype(jnp.float32) for s in range(2)]
        left = [panel_ref[part, 0, rows, pl.ds(s * WIDTH, HALF)] * masks[s] for s in range(2)]
        right = [panel_ref[part, 0, rows, pl.ds(s * WIDTH + HALF, HALF)] * masks[s] for s in range(2)]
        for s in range(2):
            first_ref[rows, pl.ds((3 * part + s) * HALF, HALF)] = left[s]
        third, fourth = halves_kernel(*right)
        first_ref[rows, pl.ds((3 * part + 2) * HALF, HALF)] = third
        last_ref[rows, pl.ds(part * HALF, HALF)] = fourth


def prepare(me, pattern, panel):
    rows = panel.shape[2]
    tile = rows // 2
    lanes = (6 * HALF, 2 * HALF)
    return pl.pallas_call(
        prepare_kernel,
        out_shape=[jax.ShapeDtypeStruct((rows, n), jnp.float32) for n in lanes],
        grid_spec=pltpu.PrefetchScalarGridSpec(
            num_scalar_prefetch=2,
            grid=(2,),
            in_specs=[pl.BlockSpec((2, 1, tile, 2 * WIDTH), lambda i, *_: (0, 0, i, 0))],
            out_specs=[pl.BlockSpec((tile, n), lambda i, *_: (i, 0)) for n in lanes],
        ),
        name="prepare",
    )(me.reshape(1), pattern, panel)


def slots_kernel(table_ref, a_ref, *refs, wanted, counts, fresh, last, joined):
    candidates, refs = refs[: 2 * sum(counts)], refs[2 * sum(counts) :]
    sum_ref, refs = (None, refs) if fresh else (refs[0], refs[1:])
    out_refs, refs = refs[: 1 + last], refs[1 + last :]
    piece_ref, high_ref, low_ref, total_ref, sems = refs
    slots = len(counts)
    tile, slot = pl.program_id(0), pl.program_id(1)
    rows, lanes = piece_ref.shape[1] // 2, piece_ref.shape[2]
    half = lanes // 2
    side = table_ref[8]

    def fetch(k, act):
        first = sum(counts[:k])
        for j in range(counts[k]):

            @pl.when((counts[k] == 1) | (table_ref[4 + wanted[k]] == j))
            def _():
                for way in range(2):
                    place = side if way == 0 else 1 - side
                    act(
                        pltpu.make_async_copy(
                            candidates[2 * (first + j) + way].at[pl.ds(way * joined * rows, rows)],
                            piece_ref.at[k, pl.ds(pl.multiple_of(place * rows, rows), rows)],
                            sems.at[k, way],
                        )
                    )

    @pl.when(tile == 0)
    def _():
        @pl.when(slot == 0)
        def _():
            for k in range(slots):
                fetch(k, lambda copy: copy.start())

        for k in range(slots):

            @pl.when(slot == k)
            def _():
                fetch(k, lambda copy: copy.wait())

        high, low = split(piece_ref[slot])
        for parts, target in ((high, high_ref), (low, low_ref)):
            target[slot, : 2 * rows] = parts
            target[slot, 2 * rows :, :half] = -parts[:, half:]
            target[slot, 2 * rows :, half:] = parts[:, :half]

    total = None
    for part in range(2):
        span = pl.ds(2 * rows * part, 2 * rows)
        term = mult_split(split(a_ref[part]), (high_ref[slot, span], low_ref[slot, span]))
        total = term if total is None else total + term

    @pl.when(slot == 0)
    def _():
        total_ref[...] = total if fresh else sum_ref[...] + total

    @pl.when(slot > 0)
    def _():
        total_ref[...] += total

    @pl.when(slot == slots - 1)
    def _():
        value = total_ref[...]
        if not last:
            out_refs[0][...] = value
            return
        siblings = halves_kernel(value[:, half - HALF : half], value[:, 2 * half - HALF :])
        if half > HALF:
            siblings = [
                jnp.concatenate(
                    [value[:, k * half + s * HALF : k * half + (s + 1) * HALF] for k in range(2)] + [siblings[s]], axis=1
                )
                for s in range(2)
            ]
        mine = table_ref[9] == 0
        out_refs[0][...] = jnp.where(mine, siblings[0], siblings[1])
        out_refs[1][...] = jnp.where(mine, siblings[1], siblings[0])


def add_slots(inverse, table, wanted, slots, total, last=False, ease=1):
    row_count = inverse.shape[2]
    counts = tuple(len(slot) for slot in slots)
    operands = [array for slot in slots for pair in slot for array in pair]
    rows, lanes = inverse.shape[3] // 8, operands[0].shape[1]
    joined = operands[0].shape[0] == 2 * rows
    fresh = total is None
    block = pl.BlockSpec((TILE, lanes), lambda i, k, t: (i, 0))
    specs = [pl.BlockSpec((2, None, TILE, 2 * rows), lambda i, k, t: (0, 0, i, t[k + wanted[0]]))]
    specs += [pl.BlockSpec(memory_space=pl.ANY)] * len(operands)
    operands = [inverse] + operands
    if not fresh:
        specs.append(block)
        operands.append(total)
    if last:
        half_block = pl.BlockSpec((TILE, lanes // 2), lambda i, k, t: (i, 0))
        out_specs = [half_block] * 2
        out_shape = [jax.ShapeDtypeStruct((row_count, lanes // 2), jnp.float32)] * 2
    else:
        out_specs, out_shape = [block], [jax.ShapeDtypeStruct((row_count, lanes), jnp.float32)]
    result = pl.pallas_call(
        functools.partial(slots_kernel, wanted=wanted, counts=counts, fresh=fresh, last=last, joined=joined),
        out_shape=out_shape,
        grid_spec=pltpu.PrefetchScalarGridSpec(
            num_scalar_prefetch=1,
            grid=(row_count // TILE, len(counts)),
            in_specs=specs,
            out_specs=out_specs,
            scratch_shapes=[
                pltpu.VMEM((len(counts), 2 * rows, lanes), jnp.float32),
                pltpu.VMEM((len(counts), 4 * rows, lanes), jnp.bfloat16),
                pltpu.VMEM((len(counts), 4 * rows, lanes), jnp.bfloat16),
                pltpu.VMEM((TILE, lanes), jnp.float32),
                pltpu.SemaphoreType.DMA((len(counts), 2)),
            ],
        ),
        compiler_params=pltpu.CompilerParams(vmem_limit_bytes=60 * 2**20),
        cost_estimate=pl.CostEstimate(
            flops=2 * 3 * row_count * 4 * rows * lanes * len(counts) // (SCALE * ease),
            bytes_accessed=4 * 4 * row_count * rows * len(counts) // (SCALE * ease),
            transcendentals=0,
        ),
        name=f"slots_{lanes}_{len(counts)}",
    )(table, *operands)
    return result if last else result[0]


def finish_kernel(mine_ref, other_ref, mask_ref, lower_ref, update_ref, term_ref):
    value = -(mine_ref[...] + other_ref[...]) * mask_ref[...]
    update_ref[...] = value
    packed = value[:, -HALF:]
    lane = lax.broadcasted_iota(jnp.int32, packed.shape, 1)
    rolled = pltpu.roll(packed, QUARTER, 1)
    turned = jnp.where(lane < QUARTER, -rolled, rolled)
    if value.shape[1] > HALF:
        turned = jnp.concatenate([-value[:, HALF : 2 * HALF], value[:, :HALF], turned], axis=1)
    total = None
    for part, right in enumerate((value, turned)):
        term = mult_split(split(lower_ref[part]), split(right))
        total = term if total is None else total + term
    term_ref[...] = total


def finish(mine, other, mask, lower):
    row_count, lanes = mine.shape
    return pl.pallas_call(
        finish_kernel,
        out_shape=[
            jax.ShapeDtypeStruct((row_count, lanes), jnp.float32),
            jax.ShapeDtypeStruct((WIDTH, lanes), jnp.float32),
        ],
        compiler_params=pltpu.CompilerParams(vmem_limit_bytes=32 * 2**20),
        cost_estimate=pl.CostEstimate(flops=0, bytes_accessed=0, transcendentals=0),
        name=f"finish_{lanes}",
    )(mine, other, mask, lower)


def assemble_kernel(first_ref, last_ref, out_ref):
    parts = halves_kernel(first_ref[:, 2 * HALF :], last_ref[...])
    for part in range(2):
        out_ref[part, :, :HALF] = first_ref[:, part * HALF : (part + 1) * HALF]
        out_ref[part, :, HALF:] = parts[part]


def assemble(first, last):
    rows = first.shape[0]
    tile = rows // 2
    return pl.pallas_call(
        assemble_kernel,
        out_shape=jax.ShapeDtypeStruct((2, rows, WIDTH), jnp.float32),
        grid=(2,),
        in_specs=[
            pl.BlockSpec((tile, 3 * HALF), lambda i: (i, 0)),
            pl.BlockSpec((tile, HALF), lambda i: (i, 0)),
        ],
        out_specs=pl.BlockSpec((2, tile, WIDTH), lambda i: (0, i, 0)),
        cost_estimate=pl.CostEstimate(flops=0, bytes_accessed=0, transcendentals=0),
        name="assemble",
    )(first, last)


def lined(ancestor_inverse, panel, diagonal_inverse, pattern):
    row_count = ancestor_inverse.shape[2]
    me = lax.axis_index("row")
    z, y = me // 2, me % 2
    sibling = lax.axis_index("leaf")
    block_count = row_count // BLOCK
    first, second = prepare(me, pattern, panel)

    def up(value, step):
        pairs = [(2 * i + j, 2 * i + 2 + j) for i in range(step, 3) for j in (0, 1)]
        return lax.ppermute(value, "row", pairs)

    def down(value, step):
        pairs = [(2 * i + j, 2 * i - 2 + j) for i in range(1, 4 - step) for j in (0, 1)]
        return lax.ppermute(value, "row", pairs)

    def across(value, places=(0, 1, 2, 3)):
        pairs = [(2 * i + j, 2 * i + 1 - j) for i in places for j in (0, 1)]
        return lax.ppermute(value, "row", pairs)

    def swap(value):
        return lax.ppermute(value, "leaf", [(0, 1), (1, 0)])

    layout = (
        (("u0",), (0, 1, 2, 3), (0, 0, 0, 0)),
        (("u1", "d1"), (1, 0, 1, 2), (1, 0, 0, 0)),
        (("u2", "d1", "d2"), (2, 2, 3, 1), (2, 1, 1, 0)),
        (("u2", "u3", "d2", "d3"), (3, 3, 0, 0), (3, 2, 0, 1)),
    )

    def by_z(values):
        return jnp.where(z == 0, values[0], jnp.where(z == 1, values[1], jnp.where(z == 2, values[2], values[3])))

    table = [by_z(sources) for _, sources, _ in layout] + [by_z(choices) for _, _, choices in layout]
    table = jnp.stack(table + [y, sibling]).astype(jnp.int32)

    local_pattern = lax.dynamic_slice_in_dim(pattern, me * block_count, block_count, 0).astype(jnp.float32)
    own_pattern = jnp.where(sibling == 0, local_pattern[:, 0], local_pattern[:, 1])
    own_mask = jnp.broadcast_to(jnp.repeat(own_pattern, BLOCK)[:, None], (row_count, HALF))

    live = {"c u0": first, "c 0": first, "t 0": second}
    live["mask"], live["wide mask"] = own_mask, jnp.concatenate([own_mask] * 3, axis=1)

    def fence():
        live.update(lax.optimization_barrier(dict(live)))

    def hop(chain, step):
        live[f"{chain} u{step}"] = up(live[f"{chain} u{max(step - 1, 0)}"], step - 1)
        live[f"{chain} d{step}"] = down(live[f"{chain} {'d' if step > 1 else 'u'}{step - 1}"], step - 1)

    def select(chain, slot):
        names, _, choices = layout[slot]
        value = live[f"{chain} {names[-1]}"]
        for j, name in enumerate(names[:-1]):
            chosen = functools.reduce(jnp.logical_or, [z == i for i in range(4) if choices[i] == j])
            value = jnp.where(chosen, live[f"{chain} {name}"], value)
        live[f"{chain} {slot}"] = value

    def cross(chain, slot):
        names, _, choices = layout[slot]
        if slot in (1, 3):
            select(chain, slot)
        if slot != 2:
            live[f"{chain} y{slot}"] = across(live[f"{chain} {slot}"])
            return
        for j, name in enumerate(names):
            places = [i for i in range(4) if choices[i] == j]
            live[f"{chain} y{slot} {name}"] = across(live[f"{chain} {name}"], places)

    def add(chain, wanted, last=False, ease=1):
        slots = []
        for k in wanted:
            if chain == "t":
                slots.append([(live[f"t {name}"],) * 2 for name in layout[k][0]])
            elif k == 2:
                slots.append([(live[f"{chain} {name}"], live[f"{chain} y{k} {name}"]) for name in layout[k][0]])
            else:
                slots.append([(live[f"{chain} {k}"], live[f"{chain} y{k}"])])
        total = live.pop(f"{chain} total", None)
        result = add_slots(ancestor_inverse, live["table"], tuple(wanted), slots, total, last, ease)
        if last:
            return result
        live[f"{chain} total"] = result

    pair = panel[:, 0]
    pair = lax.optimization_barrier((pair, first))[0]
    keep = jnp.where(sibling == 0, pair[..., :WIDTH], pair[..., WIDTH:])
    give = jnp.where(sibling == 0, pair[..., WIDTH:], pair[..., :WIDTH])

    def lower_rows():
        got = swap(give)
        even = jnp.where(sibling == 0, keep, got)
        odd = jnp.where(sibling == 0, got, keep)
        rows = jnp.stack([even, odd], axis=2).reshape(2, row_count, WIDTH)
        return jnp.transpose(rows * own_mask[None, :, :1], (0, 2, 1))

    def exchange(term, distance):
        return term + lax.ppermute(term, "row", [(i, i ^ distance) for i in range(8)])

    hop("c", 1)
    cross("c", 0)
    cross("t", 0)
    live["lower"] = lower_rows()
    live["table"] = table
    fence()
    hop("c", 2)
    cross("c", 1)
    live["t u0"] = jnp.concatenate([live.pop("t 0"), live.pop("t y0")])
    add("c", (0,))
    fence()
    hop("c", 3)
    cross("c", 2)
    add("c", (1,))
    add("t", (0,))
    fence()
    hop("t", 1)
    cross("c", 3)
    add("c", (2,))
    fence()
    hop("t", 2)
    live["mine"], live["theirs"] = add("c", (3,), last=True)
    fence()
    hop("t", 3)
    live["update c"], term = finish(live.pop("mine"), swap(live.pop("theirs")), live["wide mask"], live["lower"])
    live["term c"] = exchange(term, 1)
    add("t", (1, 2))
    fence()
    mine, theirs = add("t", (3,), last=True)
    update_last, term_last = finish(mine, swap(theirs), live["mask"], live["lower"])
    live["term c"] = exchange(exchange(live["term c"], 4), 2)
    for distance in (1, 2, 4):
        term_last = exchange(term_last, distance)

    update = assemble(live["update c"], update_last)
    total = jnp.concatenate([live["term c"], term_last], axis=1)
    real = [total[:, :HALF], total[:, 2 * HALF : 2 * HALF + QUARTER], total[:, 3 * HALF : 3 * HALF + QUARTER]]
    imag = [total[:, HALF : 2 * HALF], total[:, 2 * HALF + QUARTER : 3 * HALF], total[:, 3 * HALF + QUARTER :]]
    correction = jnp.stack([jnp.concatenate(real, axis=1), jnp.concatenate(imag, axis=1)])
    return (update, diagonal_inverse - correction[:, None])


def solution(mesh):
    in_specs = (
        P("pole", "leaf", "row", None),
        P("pole", "leaf", "row", None),
        P("pole", "leaf", None, None),
        P(),
    )
    out_specs = (P("pole", "row", "leaf"), P("pole", "leaf", None, None))
    local = lined if mesh.shape["row"] == 8 and mesh.shape["leaf"] == 2 else plain
    return jax.shard_map(local, mesh=mesh, in_specs=in_specs, out_specs=out_specs, check_vma=False)
```
